32 devices in a mesh: view: 4 (over y, core), block: 8 (over z, x).
Axes of the slice: x: 2, y: 2, z: 4, core: 2. Of those that a mesh axis runs over, the one named last changes fastest.
Arguments:
- estimate0: float32 [512, 64, 256], P('block'), may hold values from 0.5 to 1.5
- pieces: bfloat16 [4, 128, 4, 64, 256], P('view', 'block'), may hold values from 0.19921875 to 2
- dest_block: int32 [4, 128, 1], replicated, may hold values from 0 to 7; in each aligned block of 16 rows (0 to 15, 16 to 31, ..., all dimensions but the last counted through in order) at most 2 rows name the same one
- slot_index: int32 [4, 128], replicated, may hold values from 0 to 15
- psf_shift: int32 [4, 3], replicated, may hold values from -3 to 3
- psf_taps: float32 [4, 3, 21], replicated, may hold values from 0.05 to 1
- background: float32 [4], replicated, may hold values from 0.1 to 0.5
Outputs:
- estimate: float32 [512, 64, 256], P('block')
The draws below stay inside these ranges and needn't reach their ends.
Inputs may be any that keep to these rules, and one draw needn't show every extreme that they name: `dest_block`: among the 16 pieces held by one device (aligned blocks of 16 rows, views and pieces taken together), no slab is named more than 2 times.
All inputs are finite; a program needn't handle non-finite values.
Results may differ from the reference program's by a relative error of at most 0.0014.
Values may be sent and summed in bfloat16 or wider, within the bound.
A program may use at most 128 MiB of HBM per device.

```python
import math
import jax
import jax.numpy as jnp
import numpy as np
from jax import lax

NY = 64
NX = 256
SLOTS = 16
CAP = 2
SMAX = 3
ITERS = 2
TAPS = 21
HALO = 13
PZ = 4
VIEWS = 4
PIECES = 128
NZ = 512
N_BLOCK = 8


def plant(values, stream_key, smallest, largest):
    extent = values.shape
    spot = [jax.random.randint(jax.random.fold_in(stream_key, axis), (), 0, extent[axis]) for axis in range(len(extent))]
    values = values.at[tuple(spot)].set(smallest)
    longest = extent.index(max(extent))
    spot[longest] = (spot[longest] + 1) % extent[longest]
    return values.at[tuple(spot)].set(largest)


def levels(stream_key, dims, split, smallest, largest):
    factor_of, own = 1.0, jax.random.fold_in(stream_key, 6)
    for dim, shards_of in split:
        heights = jnp.exp(jax.random.uniform(jax.random.fold_in(own, dim), (shards_of,), jnp.float32, smallest / len(split), largest / len(split)))
        factor_of = factor_of * jnp.repeat(heights, dims[dim] // shards_of).reshape([-1 if axis == dim else 1 for axis in range(len(dims))])
    return factor_of


def routed_block(own_key, own, number, rows, amount, top, limit, lean):
    sequence = jax.random.permutation(own_key, amount)
    packed, usual = load_shares(amount, rows * top, limit, lean, True), load_shares(amount, rows * top, limit, lean, False)
    places = jnp.arange(amount)

    def named(tallies, turn):
        used = int((tallies > 0).sum())
        fixed = max(1, used // 4)
        moved = fixed + (places - fixed + turn * (used - fixed)) % max(1, amount - fixed)
        return jnp.zeros((amount,), jnp.int32).at[sequence[jnp.where(places < fixed, places, moved)]].set(jnp.asarray(tallies, jnp.int32))

    tallies = jnp.where(number % 4 == 0, named(packed, number // 4), named(usual, number - number // 4 - 1))
    mixed = jax.random.permutation(jax.random.fold_in(own, 3), amount)
    donor, taker = mixed[0:amount // 2 * 2:2], mixed[1:amount // 2 * 2:2]
    room = jnp.minimum(tallies[donor] - 1, limit - tallies[taker]) // 2
    room = jnp.where((donor == sequence[0]) | (taker == sequence[0]) | (tallies[taker] == 0), 0, jnp.maximum(room, 0))
    moved = jax.random.randint(jax.random.fold_in(own, 4), (amount // 2,), 0, 1 << 20) % (room + 1)
    tallies = tallies.at[donor].add(-moved).at[taker].add(moved)
    items = jnp.searchsorted(jnp.cumsum(tallies), jnp.arange(rows * top), side="right").astype(jnp.int32)
    grid = items.reshape(top, rows).T
    grid = grid[jax.random.permutation(jax.random.fold_in(own, 1), rows)]
    turn = jax.random.randint(jax.random.fold_in(own, 2), (rows, 1), 0, top)
    return jnp.take_along_axis(grid, (jnp.arange(top)[None, :] + turn) % top, axis=1)


def load_shares(number_of, total, limit, lean, full):
    loads = [(1 << 20) // math.isqrt(rank ** lean) + 1 for rank in range(1, number_of + 1)]
    largest = limit if full else min(limit, max(-(-total // number_of), total * loads[0] // sum(loads)))
    least = 1 if total - largest >= number_of - 1 else 0
    given, rest = [largest] + [least] * (number_of - 1), total - largest - least * (number_of - 1)
    while rest > 0:
        movable = [i for i in range(1, number_of) if given[i] < largest] or [i for i in range(1, number_of) if given[i] < limit]
        whole, remaining = sum([loads[i] for i in movable]), rest
        for i in movable:
            addition = min(limit - given[i], max(1, remaining * loads[i] // whole), rest)
            given[i] = given[i] + addition
            rest = rest - addition
    return np.array(given)


def setup_inputs(seed: int = 0) -> dict:
    key_of = jax.random.split(jax.random.key(seed), 8)
    estimate0 = jnp.clip(0.5 + 1.0 * jax.random.uniform(key_of[0], (NZ, NY, NX), jnp.float32) ** levels(key_of[0], (NZ, NY, NX), ((0, 8),), -0.2, 0.2), 0.5, 1.5)
    pieces = jnp.clip(0.19921875 + 1.8007812 * jax.random.uniform(key_of[1], (VIEWS, PIECES, PZ, NY, NX), jnp.float32) ** levels(key_of[1], (VIEWS, PIECES, PZ, NY, NX), ((0, 4), (1, 8)), -0.2, 0.2), 0.19921875, 2.0).astype(jnp.bfloat16)
    dest_block_keys = jax.random.split(jax.random.fold_in(key_of[2], 1), VIEWS * PIECES // SLOTS)
    dest_block_turns = jax.random.permutation(jax.random.fold_in(key_of[2], 3), VIEWS * PIECES // SLOTS)
    dest_block = jax.vmap(lambda own, number: routed_block(jax.random.fold_in(key_of[2], 2), own, number, SLOTS, N_BLOCK, 1, CAP, 2))(dest_block_keys, dest_block_turns).reshape((VIEWS, PIECES, 1))
    slot_index = plant(jax.random.randint(key_of[3], (VIEWS, PIECES), 0, SLOTS), jax.random.fold_in(key_of[3], 1), 0, SLOTS - 1).astype(jnp.int32)
    psf_shift = plant(jax.random.randint(key_of[4], (VIEWS, 3), 0 - SMAX, SMAX + 1), jax.random.fold_in(key_of[4], 1), 0 - SMAX, SMAX).astype(jnp.int32)
    psf_taps = jnp.clip(jnp.exp(jax.random.uniform(key_of[5], (VIEWS, 3, TAPS), jnp.float32, math.log(0.05), math.log(1.0))), 0.05, 1.0)
    background = jnp.clip(jnp.exp(jax.random.uniform(key_of[6], (VIEWS,), jnp.float32, math.log(0.1), math.log(0.5))), 0.1, 0.5)
    return {"estimate0": estimate0, "pieces": pieces, "dest_block": dest_block, "slot_index": slot_index, "psf_shift": psf_shift, "psf_taps": psf_taps, "background": background}


HIGHEST = lax.Precision.HIGHEST


def band_matrix(kernel, shift, row_count, column_count, lead_offset):
    tap_count = kernel.shape[0]
    radius = (tap_count - 1) // 2
    difference = (lax.broadcasted_iota(jnp.int32, (row_count, column_count), 1)
                  - lax.broadcasted_iota(jnp.int32, (row_count, column_count), 0)
                  - lead_offset - shift + radius)
    tap_hits = difference[:, :, None] == jnp.arange(tap_count, dtype=jnp.int32)[None, None, :]
    return jnp.sum(jnp.where(tap_hits, kernel[None, None, :], 0.0), axis=2)


def column_sums(kernel, shift, length):
    tap_count = kernel.shape[-1]
    radius = (tap_count - 1) // 2
    source = (jnp.arange(length, dtype=jnp.int32)[None, :, None] - shift[:, None, None]
              - jnp.arange(tap_count, dtype=jnp.int32)[None, None, :] + radius)
    inside = (source >= 0) & (source < length)
    return jnp.sum(jnp.where(inside, kernel[:, None, :], 0.0), axis=2)


def shift_sum(volume, kernel, shift, direction):
    length = volume.shape[0]
    tap_count = kernel.shape[0]
    radius = (tap_count - 1) // 2
    padded = jnp.pad(volume, [(HALO, HALO)] + [(0, 0)] * (volume.ndim - 1))
    result = jnp.zeros_like(volume)
    for tap in range(tap_count):
        start = (HALO + direction * (shift + tap - radius)).astype(jnp.int32)
        result = result + kernel[tap] * lax.dynamic_slice_in_dim(padded, start, length, 0)
    return result


def blur_plane(volume, band_rows, band_columns):
    along_rows = jnp.einsum('yv,zvx->zyx', band_rows, volume, precision=HIGHEST)
    return jnp.einsum('zyv,xv->zyx', along_rows, band_columns, precision=HIGHEST)


def adjoint_plane(volume, band_rows, band_columns):
    along_rows = jnp.einsum('vy,zvx->zyx', band_rows, volume, precision=HIGHEST)
    return jnp.einsum('zyv,vx->zyx', along_rows, band_columns, precision=HIGHEST)


def reference(estimate0, pieces, dest_block, slot_index, psf_shift, psf_taps, background):
    kernel = psf_taps / jnp.sum(psf_taps, axis=2, keepdims=True)
    slot_total = N_BLOCK * SLOTS
    global_slot = (dest_block[:, :, 0] * SLOTS + slot_index).astype(jnp.int32)
    averages = []
    band_list = []
    depth_weights = []
    for viewer in range(VIEWS):
        counts = jax.ops.segment_sum(jnp.ones((PIECES,), jnp.int32), global_slot[viewer], num_segments=slot_total)
        placed = jax.ops.segment_sum(pieces[viewer].astype(jnp.float32).reshape(PIECES, PZ * NY * NX),
                                     global_slot[viewer], num_segments=slot_total)
        average = placed / jnp.maximum(counts, 1).astype(jnp.float32)[:, None]
        averages.append(average.reshape(NZ, NY, NX))
        plane_mask = jnp.repeat((counts > 0).astype(jnp.float32), PZ)
        depth_weights.append(shift_sum(plane_mask, kernel[viewer, 0], psf_shift[viewer, 0], -1))
        band_list.append((band_matrix(kernel[viewer, 1], psf_shift[viewer, 1], NY, NY, 0),
                          band_matrix(kernel[viewer, 2], psf_shift[viewer, 2], NX, NX, 0)))
    weight_depth = jnp.stack(depth_weights)
    weight_rows = column_sums(kernel[:, 1], psf_shift[:, 1], NY)
    weight_columns = column_sums(kernel[:, 2], psf_shift[:, 2], NX)
    weight = jnp.einsum('vz,vy,vx->zyx', weight_depth, weight_rows, weight_columns, precision=HIGHEST)
    floor_weight = jnp.maximum(weight, 1.0)
    estimate = estimate0
    for iteration in range(ITERS):
        summed = jnp.zeros_like(estimate)
        for viewer in range(VIEWS):
            band_rows, band_columns = band_list[viewer]
            blurred = blur_plane(shift_sum(estimate, kernel[viewer, 0], psf_shift[viewer, 0], 1),
                                 band_rows, band_columns) + background[viewer]
            quotient = averages[viewer] / blurred
            summed = summed + shift_sum(adjoint_plane(quotient, band_rows, band_columns),
                                        kernel[viewer, 0], psf_shift[viewer, 0], -1)
        estimate = estimate * summed / floor_weight
    return estimate
```

```python
import functools

import jax
import jax.numpy as jnp
from jax import lax
from jax.experimental import pallas as pl
from jax.experimental.pallas import tpu as pltpu
from jax.sharding import PartitionSpec as P

CAP = 2
ITERS = 2
HALO = 13
EDGE = 16
CORES = 2
LANES = 128

HIGHEST = lax.Precision.HIGHEST
BF16 = jnp.bfloat16
F32 = jnp.float32


def band_matrix(kernel, shift, row_count, column_count, lead_offset):
    tap_count = kernel.shape[0]
    radius = (tap_count - 1) // 2
    difference = (
        lax.broadcasted_iota(jnp.int32, (row_count, column_count), 1)
        - lax.broadcasted_iota(jnp.int32, (row_count, column_count), 0)
        - lead_offset
        - shift
        + radius
    )
    band = jnp.zeros((row_count, column_count), F32)
    for tap in range(tap_count):
        band = jnp.where(difference == tap, kernel[tap], band)
    return band


def column_sums(kernel, shift, length):
    tap_count = kernel.shape[-1]
    radius = (tap_count - 1) // 2
    source = (
        jnp.arange(length, dtype=jnp.int32)[None, :, None]
        - shift[:, None, None]
        - jnp.arange(tap_count, dtype=jnp.int32)[None, None, :]
        + radius
    )
    inside = (source >= 0) & (source < length)
    return jnp.sum(jnp.where(inside, kernel[:, None, :], 0.0), axis=2)


def copy_body(index_ref, piece_ref, out_ref):
    out_ref[...] = piece_ref[...]


def pick_pieces(pieces, index):
    block = (1,) + pieces.shape[1:]
    return pl.pallas_call(
        copy_body,
        grid_spec=pltpu.PrefetchScalarGridSpec(
            num_scalar_prefetch=1,
            grid=(index.shape[0],),
            in_specs=[pl.BlockSpec(block, lambda i, s: (s[i], 0, 0))],
            out_specs=pl.BlockSpec(block, lambda i, s: (i, 0, 0)),
        ),
        out_shape=jax.ShapeDtypeStruct((index.shape[0],) + pieces.shape[1:], pieces.dtype),
        name="pick_pieces",
    )(index, pieces)


def place_body(order_ref, start_ref, scale_ref, incoming_ref, out_ref):
    view, slot = pl.program_id(0), pl.program_id(1)
    out_ref[...] = jnp.zeros_like(out_ref)

    def add(k, carry):
        out_ref[0, 0] += incoming_ref[0, order_ref[view, k]].astype(F32)
        return carry

    lax.fori_loop(start_ref[view, slot], start_ref[view, slot + 1], add, 0)
    out_ref[...] = out_ref[...] * scale_ref[view, slot]


def place_pieces(incoming, order, start, scale):
    views, slots = scale.shape
    tail = incoming.shape[2:]
    return pl.pallas_call(
        place_body,
        grid=(views, slots),
        in_specs=[
            pl.BlockSpec(memory_space=pltpu.SMEM),
            pl.BlockSpec(memory_space=pltpu.SMEM),
            pl.BlockSpec(memory_space=pltpu.SMEM),
            pl.BlockSpec((1,) + incoming.shape[1:], lambda v, t: (v, 0, 0, 0)),
        ],
        out_specs=pl.BlockSpec((1, 1) + tail, lambda v, t: (v, t, 0, 0)),
        out_shape=jax.ShapeDtypeStruct((views, slots) + tail, F32),
        compiler_params=pltpu.CompilerParams(vmem_limit_bytes=48 * 2**20),
        name="place_pieces",
    )(order, start, scale, incoming)


def split_columns(volume):
    return jnp.stack(jnp.split(volume, volume.shape[-1] // LANES, axis=-1))


def take_rows(ref, y, rows):
    halves, total = ref.shape[:2]
    return jnp.concatenate(
        [ref[h, pl.ds(y, total // rows, stride=rows), :].astype(BF16) for h in range(halves)],
        axis=1,
    )


def forward_body(offset_ref, depth_ref, rows_ref, columns_ref, volume_ref, out_ref, source, middle):
    view = pl.program_id(0)
    halves, depth_in, rows, _ = volume_ref.shape
    depth = out_ref.shape[1]

    @pl.when(view == 0)
    def _():
        for h in range(halves):

            def widen(z, carry):
                source[h, pl.ds(pl.multiple_of(z * rows, rows), rows), :] = volume_ref[h, z].astype(F32)
                return carry

            lax.fori_loop(0, depth_in, widen, 0, unroll=8)

    def row(y, carry):
        column = take_rows(source, y, rows)
        blurred = jnp.dot(depth_ref[0], column, preferred_element_type=F32).astype(BF16)
        blurred = jnp.dot(blurred, columns_ref[0], preferred_element_type=F32)
        for h in range(halves):
            middle[h, pl.ds(y, depth, stride=rows), :] = blurred[:, h * LANES : (h + 1) * LANES]
        return carry

    lax.fori_loop(0, rows, row, 0, unroll=8)

    def plane(z, carry):
        span = pl.ds(pl.multiple_of(z * rows, rows), rows)
        cells = jnp.concatenate([middle[h, span, :].astype(BF16) for h in range(halves)], axis=1)
        out_ref[0, z] = (
            jnp.dot(rows_ref[0], cells, preferred_element_type=F32) + offset_ref[view]
        )
        return carry

    lax.fori_loop(0, depth, plane, 0, unroll=8)


def forward(volume, offset, depth_bands, row_bands, column_bands):
    views, depth = depth_bands.shape[:2]
    halves, depth_in, rows, _ = volume.shape
    width = halves * LANES
    matrix = lambda a: pl.BlockSpec((1,) + a.shape[1:], lambda v: (v, 0, 0))
    return pl.pallas_call(
        forward_body,
        grid=(views,),
        in_specs=[
            pl.BlockSpec(memory_space=pltpu.SMEM),
            matrix(depth_bands),
            matrix(row_bands),
            matrix(column_bands),
            pl.BlockSpec(volume.shape, lambda v: (0, 0, 0, 0)),
        ],
        out_specs=pl.BlockSpec((1, depth, rows, width), lambda v: (v, 0, 0, 0)),
        out_shape=jax.ShapeDtypeStruct((views, depth, rows, width), F32),
        scratch_shapes=[
            pltpu.VMEM((halves, depth_in * rows, LANES), F32),
            pltpu.VMEM((halves, depth * rows, LANES), F32),
        ],
        compiler_params=pltpu.CompilerParams(vmem_limit_bytes=48 * 2**20),
        cost_estimate=pl.CostEstimate(
            flops=2 * views * depth * rows * width * (depth_in + rows + width) * 4,
            bytes_accessed=4 * (views * depth + depth_in) * rows * width,
            transcendentals=0,
        ),
        name="forward_blur",
    )(offset, depth_bands, row_bands, column_bands, volume)


def backward_body(depth_ref, rows_ref, columns_ref, average_ref, blurred_ref, out_ref, middle):
    view = pl.program_id(0)
    _, depth, rows, _ = average_ref.shape
    halves = out_ref.shape[0]
    depth_out = out_ref.shape[1] // rows

    def plane(z, carry):
        quotient = (average_ref[0, z] / blurred_ref[0, z]).astype(BF16)
        cells = jnp.dot(rows_ref[0], quotient, preferred_element_type=F32)
        span = pl.ds(pl.multiple_of(z * rows, rows), rows)
        for h in range(halves):
            middle[h, span, :] = cells[:, h * LANES : (h + 1) * LANES]
        return carry

    lax.fori_loop(0, depth, plane, 0, unroll=8)

    def spread(y):
        column = take_rows(middle, y, rows)
        column = jnp.dot(column, columns_ref[0], preferred_element_type=F32).astype(BF16)
        return jnp.dot(depth_ref[0], column, preferred_element_type=F32)

    @pl.when(view == 0)
    def _():
        def row(y, carry):
            cells = spread(y)
            for h in range(halves):
                out_ref[h, pl.ds(y, depth_out, stride=rows), :] = cells[:, h * LANES : (h + 1) * LANES]
            return carry

        lax.fori_loop(0, rows, row, 0, unroll=8)

    @pl.when(view > 0)
    def _():
        def row(y, carry):
            cells = spread(y)
            for h in range(halves):
                out_ref[h, pl.ds(y, depth_out, stride=rows), :] += cells[:, h * LANES : (h + 1) * LANES]
            return carry

        lax.fori_loop(0, rows, row, 0, unroll=8)


def backward(average, blurred, depth_bands, row_bands, column_bands):
    views, depth_out = depth_bands.shape[:2]
    _, depth, rows, width = blurred.shape
    halves = width // LANES
    matrix = lambda a: pl.BlockSpec((1,) + a.shape[1:], lambda v: (v, 0, 0))
    whole = pl.BlockSpec((1, depth, rows, width), lambda v: (v, 0, 0, 0))
    out = pl.pallas_call(
        backward_body,
        grid=(views,),
        in_specs=[matrix(depth_bands), matrix(row_bands), matrix(column_bands), whole, whole],
        out_specs=pl.BlockSpec((halves, depth_out * rows, LANES), lambda v: (0, 0, 0)),
        out_shape=jax.ShapeDtypeStruct((halves, depth_out * rows, LANES), F32),
        scratch_shapes=[pltpu.VMEM((halves, depth * rows, LANES), F32)],
        compiler_params=pltpu.CompilerParams(vmem_limit_bytes=56 * 2**20),
        name="backward_blur",
    )(depth_bands, row_bands, column_bands, average, blurred)
    return out.reshape(halves, depth_out, rows, LANES)


def shards(estimate0, pieces, dest_block, slot_index, psf_shift, psf_taps, background):
    block_count = lax.axis_size("block")
    view_count = lax.axis_size("view")
    my_view = lax.axis_index("view")
    my_block = lax.axis_index("block")
    slab_depth, plane_rows, plane_columns = estimate0.shape
    slot_count = pieces.shape[1]
    piece_depth = pieces.shape[2]
    chips = view_count // CORES
    my_core = lax.rem(my_view, CORES)

    def of_own_views(cells):
        return jnp.concatenate(
            [
                lax.dynamic_slice_in_dim(cells, lax.rem(my_view + CORES * hop, view_count), 1, 0)
                for hop in range(chips)
            ]
        )

    targets = dest_block[:, :, 0].reshape(view_count, block_count, slot_count)
    slots = slot_index.reshape(view_count, block_count, slot_count)
    earlier = lax.broadcasted_iota(jnp.int32, (slot_count, slot_count), 1) < lax.broadcasted_iota(
        jnp.int32, (slot_count, slot_count), 0
    )
    here = lax.dynamic_slice(targets, (my_view, my_block, 0), (1, 1, slot_count))[0, 0]
    here_rank = jnp.sum(((here[:, None] == here[None, :]) & earlier).astype(jnp.int32), axis=1)
    buffer_slots = jnp.arange(block_count * CAP, dtype=jnp.int32)
    hit = buffer_slots[:, None] == (here * CAP + here_rank)[None, :]
    pick = jnp.sum(
        jnp.where(hit, lax.broadcasted_iota(jnp.int32, hit.shape, 1), 0), axis=1
    )
    outgoing = pick_pieces(
        pieces.reshape(slot_count, piece_depth * plane_rows, plane_columns), pick
    ).reshape(block_count, CAP, piece_depth * plane_rows, plane_columns)
    incoming = lax.all_to_all(outgoing, "block", split_axis=0, concat_axis=0, tiled=True)
    incoming = incoming.reshape(block_count * CAP, piece_depth * plane_rows, plane_columns)
    arrived = [incoming]
    for hop in range(1, chips):
        arrived.append(
            lax.ppermute(
                incoming,
                "view",
                [((v + CORES * hop) % view_count, v) for v in range(view_count)],
            )
        )
    arrived = jnp.stack(arrived)

    view_targets = of_own_views(targets)
    view_slots = of_own_views(slots)
    ranks = jnp.sum(
        ((view_targets[..., :, None] == view_targets[..., None, :]) & earlier).astype(jnp.int32),
        axis=-1,
    )
    column = jnp.where(
        view_targets == my_block,
        lax.broadcasted_iota(jnp.int32, view_targets.shape, 1) * CAP + ranks,
        -1,
    )
    matches = column[..., None] == buffer_slots
    slot_of = jnp.sum(jnp.where(matches, view_slots[..., None] + 1, 0), axis=(1, 2)) - 1
    slot_of = jnp.where(slot_of < 0, slot_count, slot_of)
    before = (slot_of[:, None, :] < slot_of[:, :, None]) | (
        (slot_of[:, None, :] == slot_of[:, :, None])
        & (buffer_slots[None, None, :] < buffer_slots[None, :, None])
    )
    position = jnp.sum(before.astype(jnp.int32), axis=2)
    order = jnp.sum(
        jnp.where(
            position[:, None, :] == buffer_slots[None, :, None], buffer_slots[None, None, :], 0
        ),
        axis=2,
    )
    thresholds = jnp.arange(slot_count + 1, dtype=jnp.int32)
    start = jnp.sum((slot_of[:, None, :] < thresholds[None, :, None]).astype(jnp.int32), axis=2)
    slab_counts = start[:, 1:] - start[:, :-1]
    scale = 1.0 / jnp.maximum(slab_counts, 1).astype(F32)
    average = place_pieces(arrived, order, start, scale)
    average = average.reshape(chips, slab_depth, plane_rows, plane_columns)

    kernel = psf_taps / jnp.sum(psf_taps, axis=2, keepdims=True)
    own_kernel = of_own_views(kernel)
    own_shift = of_own_views(psf_shift)
    own_offset = of_own_views(background)
    wide_depth = slab_depth + 2 * EDGE

    def bands(one_kernel, one_shift):
        return (
            band_matrix(one_kernel[0], one_shift[0], slab_depth, wide_depth, EDGE).astype(BF16),
            band_matrix(one_kernel[1], one_shift[1], plane_rows, plane_rows, 0).astype(BF16),
            band_matrix(one_kernel[2], one_shift[2], plane_columns, plane_columns, 0).astype(BF16),
        )

    depth_bands, row_bands, column_bands = jax.vmap(bands)(own_kernel, own_shift)
    depth_back = jnp.swapaxes(depth_bands, 1, 2)
    rows_back = jnp.swapaxes(row_bands, 1, 2)
    columns_forward = jnp.swapaxes(column_bands, 1, 2)

    global_slot = targets * slot_count + slots
    slot_total = block_count * slot_count
    counts_all = jnp.sum(
        (
            global_slot.reshape(view_count, slot_total)[:, :, None]
            == jnp.arange(slot_total, dtype=jnp.int32)[None, None, :]
        ).astype(jnp.int32),
        axis=1,
    )
    plane_mask = jnp.repeat((counts_all > 0).astype(F32), piece_depth, axis=1)
    padded_mask = jnp.pad(plane_mask, ((0, 0), (HALO, HALO)))
    window = lax.dynamic_slice_in_dim(padded_mask, my_block * slab_depth, slab_depth + 2 * HALO, 1)

    def depth_adjoint(one_kernel, one_shift):
        return band_matrix(one_kernel, one_shift, slab_depth + 2 * HALO, slab_depth, -HALO).T

    adjoint_all = jax.vmap(depth_adjoint)(kernel[:, 0], psf_shift[:, 0])
    weight_depth = jnp.einsum("vze,ve->vz", adjoint_all, window, precision=HIGHEST)
    weight_rows = column_sums(kernel[:, 1], psf_shift[:, 1], plane_rows)
    weight_columns = column_sums(kernel[:, 2], psf_shift[:, 2], plane_columns)
    weight_columns = lax.dynamic_slice_in_dim(weight_columns, my_core * LANES, LANES, 1)
    weight = 0.0
    for view in range(view_count):
        weight = weight + (
            weight_depth[view][:, None, None]
            * (weight_rows[view][:, None] * weight_columns[view][None, :])[None]
        )
    floor_weight = jnp.maximum(weight, 1.0)

    up = [(i, i + 1) for i in range(block_count - 1)]
    down = [(i + 1, i) for i in range(block_count - 1)]
    swap = [(v, v + 1 - 2 * (v % CORES)) for v in range(view_count)]

    def widen(cells):
        low = lax.ppermute(cells[slab_depth - HALO :], "block", up)
        high = lax.ppermute(cells[:HALO], "block", down)
        blank = jnp.zeros((EDGE - HALO,) + cells.shape[1:], cells.dtype)
        return jnp.concatenate([blank, low, cells, high, blank], axis=0)

    def pair(mine):
        theirs = lax.ppermute(mine, "view", swap)
        first = my_core == 0
        return jnp.where(first, mine, theirs), jnp.where(first, theirs, mine)

    def half(cells, core):
        return lax.dynamic_index_in_dim(cells, core, 0, keepdims=False)

    share = lax.dynamic_slice_in_dim(estimate0, my_core * LANES, LANES, 2)
    for iteration in range(ITERS):
        if iteration == 0:
            wide = split_columns(widen(estimate0.astype(BF16)))
        else:
            wide = jnp.stack(pair(widen(share.astype(BF16))))
        blurred = forward(wide, own_offset, depth_bands, row_bands, columns_forward)
        spread = backward(average, blurred, depth_back, rows_back, column_bands)
        total = half(spread, my_core) + lax.ppermute(half(spread, 1 - my_core), "view", swap)
        from_low = lax.ppermute(
            total[slab_depth + EDGE : slab_depth + EDGE + HALO], "block", up
        )
        from_high = lax.ppermute(total[EDGE - HALO : EDGE], "block", down)
        summed = total[EDGE : EDGE + slab_depth]
        summed = summed + jnp.concatenate(
            [
                from_low,
                jnp.zeros((slab_depth - 2 * HALO,) + from_low.shape[1:], F32),
                from_high,
            ],
            axis=0,
        )
        share = share * summed / floor_weight
    return jnp.concatenate(pair(share), axis=2)


def solution(mesh):
    return jax.shard_map(
        shards,
        mesh=mesh,
        in_specs=(
            P("block", None, None),
            P("view", "block", None, None, None),
            P(),
            P(),
            P(),
            P(),
            P(),
        ),
        out_specs=P("block", None, None),
        check_vma=False,
    )
```

```python
import jax
import jax.numpy as jnp
from jax import lax
from jax.experimental import pallas as pl
from jax.experimental.pallas import tpu as pltpu
from jax.sharding import PartitionSpec as P

CAP = 2
ITERS = 2
HALO = 13
EDGE = 16
CORES = 2
LANES = 128

HIGHEST = lax.Precision.HIGHEST
BF16 = jnp.bfloat16
F32 = jnp.float32


def band_matrix(kernel, shift, row_count, column_count, lead_offset):
    tap_count = kernel.shape[0]
    radius = (tap_count - 1) // 2
    difference = (
        lax.broadcasted_iota(jnp.int32, (row_count, column_count), 1)
        - lax.broadcasted_iota(jnp.int32, (row_count, column_count), 0)
        - lead_offset
        - shift
        + radius
    )
    band = jnp.zeros((row_count, column_count), F32)
    for tap in range(tap_count):
        band = jnp.where(difference == tap, kernel[tap], band)
    return band


def column_sums(kernel, shift, length):
    tap_count = kernel.shape[-1]
    radius = (tap_count - 1) // 2
    source = (
        jnp.arange(length, dtype=jnp.int32)[None, :, None]
        - shift[:, None, None]
        - jnp.arange(tap_count, dtype=jnp.int32)[None, None, :]
        + radius
    )
    inside = (source >= 0) & (source < length)
    return jnp.sum(jnp.where(inside, kernel[:, None, :], 0.0), axis=2)


def pick_body(index_ref, piece_ref, out_ref, sems):
    copies = [
        pltpu.make_async_copy(piece_ref.at[index_ref[i]], out_ref.at[i], sems.at[i])
        for i in range(out_ref.shape[0])
    ]
    for copy in copies:
        copy.start()
    for copy in copies:
        copy.wait()


def pick_pieces(pieces, index):
    count = index.shape[0]
    return pl.pallas_call(
        pick_body,
        in_specs=[pl.BlockSpec(memory_space=pltpu.SMEM), pl.BlockSpec(memory_space=pl.ANY)],
        out_specs=pl.BlockSpec(memory_space=pl.ANY),
        out_shape=jax.ShapeDtypeStruct((count,) + pieces.shape[1:], pieces.dtype),
        scratch_shapes=[pltpu.SemaphoreType.DMA((count,))],
        name="pick_pieces",
    )(index, pieces)


def place_body(order_ref, start_ref, scale_ref, incoming_ref, out_ref):
    view, step = pl.program_id(0), pl.program_id(1)
    group = out_ref.shape[1]
    for i in range(group):
        slot = step * group + i
        out_ref[0, i] = jnp.zeros(out_ref.shape[2:], F32)

        def add(k, carry):
            out_ref[0, i] += incoming_ref[0, order_ref[view, k]].astype(F32)
            return carry

        lax.fori_loop(start_ref[view, slot], start_ref[view, slot + 1], add, 0)
        out_ref[0, i] = out_ref[0, i] * scale_ref[view, slot]


def place_pieces(incoming, order, start, scale):
    views, slots = scale.shape
    tail = incoming.shape[2:]
    group = 4 if slots % 4 == 0 else 1
    return pl.pallas_call(
        place_body,
        grid=(views, slots // group),
        in_specs=[
            pl.BlockSpec(memory_space=pltpu.SMEM),
            pl.BlockSpec(memory_space=pltpu.SMEM),
            pl.BlockSpec(memory_space=pltpu.SMEM),
            pl.BlockSpec((1,) + incoming.shape[1:], lambda v, t: (v, 0, 0, 0)),
        ],
        out_specs=pl.BlockSpec((1, group) + tail, lambda v, t: (v, t, 0, 0)),
        out_shape=jax.ShapeDtypeStruct((views, slots) + tail, F32),
        compiler_params=pltpu.CompilerParams(vmem_limit_bytes=48 * 2**20),
        name="place_pieces",
    )(order, start, scale, incoming)


def split_columns(volume):
    return jnp.stack(jnp.split(volume, volume.shape[-1] // LANES, axis=-1))


def take_rows(ref, y, rows):
    halves, total = ref.shape[:2]
    return jnp.concatenate(
        [ref[h, pl.ds(y, total // rows, stride=rows), :].astype(BF16) for h in range(halves)],
        axis=1,
    )


def blur_depth_columns(depth_ref, columns_ref, volume_ref, source, middle):
    halves, depth_in, rows, _ = volume_ref.shape
    views = columns_ref.shape[0]
    depth = depth_ref.shape[0] // views
    for h in range(halves):

        def widen(z, carry):
            span = pl.ds(pl.multiple_of(z * rows, rows), rows)
            source[h, span, :] = volume_ref[h, z].astype(F32)
            return carry

        lax.fori_loop(0, depth_in, widen, 0, unroll=8)

    def row(y, carry):
        column = take_rows(source, y, rows)
        deep = jnp.dot(depth_ref[...], column, preferred_element_type=F32).astype(BF16)
        for v in range(views):
            cells = jnp.dot(
                deep[v * depth : (v + 1) * depth], columns_ref[v], preferred_element_type=F32
            )
            for h in range(halves):
                middle[v, h, pl.ds(y, depth, stride=rows), :] = cells[:, h * LANES : (h + 1) * LANES]
        return carry

    lax.fori_loop(0, rows, row, 0, unroll=4)


def spread_quotients(
    offset_ref, depth_ref, rows_ref, rows_back_ref, columns_ref, average_ref, middle, turned, out_ref
):
    views, depth, rows, _ = average_ref.shape
    halves = out_ref.shape[0]
    depth_out = out_ref.shape[1] // rows

    def plane(z, carry):
        span = pl.ds(pl.multiple_of(z * rows, rows), rows)
        for v in range(views):
            cells = jnp.concatenate(
                [middle[v, h, span, :].astype(BF16) for h in range(halves)], axis=1
            )
            blurred = jnp.dot(rows_ref[v], cells, preferred_element_type=F32) + offset_ref[v]
            quotient = (average_ref[v, z] / blurred).astype(BF16)
            cells = jnp.dot(rows_back_ref[v], quotient, preferred_element_type=F32)
            for h in range(halves):
                turned[v, h, span, :] = cells[:, h * LANES : (h + 1) * LANES]
        return carry

    lax.fori_loop(0, depth, plane, 0, unroll=4)

    def row(y, carry):
        columns = [
            jnp.dot(
                take_rows(turned.at[v], y, rows), columns_ref[v], preferred_element_type=F32
            ).astype(BF16)
            for v in range(views)
        ]
        cells = jnp.dot(
            depth_ref[...], jnp.concatenate(columns, axis=0), preferred_element_type=F32
        )
        for h in range(halves):
            out_ref[h, pl.ds(y, depth_out, stride=rows), :] = cells[:, h * LANES : (h + 1) * LANES]
        return carry

    lax.fori_loop(0, rows, row, 0, unroll=4)


def whole_step_body(
    offset_ref, depth_ref, depth_back_ref, rows_ref, rows_back_ref, columns_ref, columns_back_ref,
    average_ref, volume_ref, out_ref, source, middle,
):
    blur_depth_columns(depth_ref, columns_ref, volume_ref, source, middle)
    spread_quotients(
        offset_ref, depth_back_ref, rows_ref, rows_back_ref, columns_back_ref, average_ref,
        middle, middle, out_ref,
    )


IN_SMEM = pl.BlockSpec(memory_space=pltpu.SMEM)
IN_VMEM = pl.BlockSpec(memory_space=pltpu.VMEM)
ROOM = pltpu.CompilerParams(vmem_limit_bytes=60 * 2**20)


def first_half(volume, bands):
    halves, depth_in, rows, _ = volume.shape
    views = bands["columns"].shape[0]
    depth = bands["depth"].shape[0] // views
    shape = (views, halves, depth * rows, LANES)
    width = halves * LANES
    return pl.pallas_call(
        blur_depth_columns,
        in_specs=[IN_VMEM] * 3,
        out_specs=[IN_VMEM] * 2,
        out_shape=[
            jax.ShapeDtypeStruct((halves, depth_in * rows, LANES), F32),
            jax.ShapeDtypeStruct(shape, F32),
        ],
        compiler_params=ROOM,
        cost_estimate=pl.CostEstimate(
            flops=8 * views * depth * rows * width * (depth_in + width),
            bytes_accessed=4 * (views * depth + depth_in) * rows * width,
            transcendentals=0,
        ),
        name="blur_depth_columns",
    )(bands["depth"], bands["columns"], volume)[1]


def second_half(middle, average, bands):
    views, halves, _, _ = middle.shape
    rows = average.shape[2]
    depth_out = bands["depth_back"].shape[0]
    return pl.pallas_call(
        spread_quotients_apart,
        in_specs=[IN_SMEM] + [IN_VMEM] * 6,
        out_specs=IN_VMEM,
        out_shape=jax.ShapeDtypeStruct((halves, depth_out * rows, LANES), F32),
        scratch_shapes=[pltpu.VMEM(middle.shape, F32)],
        compiler_params=ROOM,
        name="spread_quotients",
    )(
        bands["offset"], bands["depth_back"], bands["rows"], bands["rows_back"],
        bands["columns_back"], average, middle,
    ).reshape(halves, depth_out, rows, LANES)


def spread_quotients_apart(
    offset_ref, depth_ref, rows_ref, rows_back_ref, columns_ref, average_ref, middle, out_ref, turned
):
    spread_quotients(
        offset_ref, depth_ref, rows_ref, rows_back_ref, columns_ref, average_ref, middle, turned,
        out_ref,
    )


def whole_step(volume, average, bands):
    halves, depth_in, rows, _ = volume.shape
    views, depth = average.shape[:2]
    depth_out = bands["depth_back"].shape[0]
    return pl.pallas_call(
        whole_step_body,
        in_specs=[IN_SMEM] + [IN_VMEM] * 8,
        out_specs=IN_VMEM,
        out_shape=jax.ShapeDtypeStruct((halves, depth_out * rows, LANES), F32),
        scratch_shapes=[
            pltpu.VMEM((halves, depth_in * rows, LANES), F32),
            pltpu.VMEM((views, halves, depth * rows, LANES), F32),
        ],
        compiler_params=ROOM,
        name="whole_step",
    )(
        bands["offset"], bands["depth"], bands["depth_back"], bands["rows"], bands["rows_back"],
        bands["columns"], bands["columns_back"], average, volume,
    ).reshape(halves, depth_out, rows, LANES)


def shards(estimate0, pieces, dest_block, slot_index, psf_shift, psf_taps, background):
    block_count = lax.axis_size("block")
    view_count = lax.axis_size("view")
    my_view = lax.axis_index("view")
    my_block = lax.axis_index("block")
    slab_depth, plane_rows, plane_columns = estimate0.shape
    slot_count = pieces.shape[1]
    piece_depth = pieces.shape[2]
    chips = view_count // CORES
    my_core = lax.rem(my_view, CORES)

    def of_own_views(cells):
        return jnp.concatenate(
            [
                lax.dynamic_slice_in_dim(cells, lax.rem(my_view + CORES * hop, view_count), 1, 0)
                for hop in range(chips)
            ]
        )

    targets = dest_block[:, :, 0].reshape(view_count, block_count, slot_count)
    slots = slot_index.reshape(view_count, block_count, slot_count)
    earlier = lax.broadcasted_iota(jnp.int32, (slot_count, slot_count), 1) < lax.broadcasted_iota(
        jnp.int32, (slot_count, slot_count), 0
    )
    here = lax.dynamic_slice(targets, (my_view, my_block, 0), (1, 1, slot_count))[0, 0]
    here_rank = jnp.sum(((here[:, None] == here[None, :]) & earlier).astype(jnp.int32), axis=1)
    buffer_slots = jnp.arange(block_count * CAP, dtype=jnp.int32)
    hit = buffer_slots[:, None] == (here * CAP + here_rank)[None, :]
    pick = jnp.sum(
        jnp.where(hit, lax.broadcasted_iota(jnp.int32, hit.shape, 1), 0), axis=1
    )
    outgoing = pick_pieces(
        pieces.reshape(slot_count, piece_depth * plane_rows, plane_columns), pick
    ).reshape(block_count, CAP, piece_depth * plane_rows, plane_columns)
    parts = [[] for _ in range(chips)]
    for part in range(CAP):
        incoming = lax.all_to_all(outgoing[:, part], "block", split_axis=0, concat_axis=0, tiled=True)
        parts[0].append(incoming)
        for hop in range(1, chips):
            parts[hop].append(
                lax.ppermute(
                    incoming,
                    "view",
                    [((v + CORES * hop) % view_count, v) for v in range(view_count)],
                )
            )
    arrived = jnp.stack([jnp.concatenate(group, axis=0) for group in parts])

    view_targets = of_own_views(targets)
    view_slots = of_own_views(slots)
    ranks = jnp.sum(
        ((view_targets[..., :, None] == view_targets[..., None, :]) & earlier).astype(jnp.int32),
        axis=-1,
    )
    column = jnp.where(
        view_targets == my_block,
        ranks * block_count + lax.broadcasted_iota(jnp.int32, view_targets.shape, 1),
        -1,
    )
    matches = column[..., None] == buffer_slots
    slot_of = jnp.sum(jnp.where(matches, view_slots[..., None] + 1, 0), axis=(1, 2)) - 1
    slot_of = jnp.where(slot_of < 0, slot_count, slot_of)
    before = (slot_of[:, None, :] < slot_of[:, :, None]) | (
        (slot_of[:, None, :] == slot_of[:, :, None])
        & (buffer_slots[None, None, :] < buffer_slots[None, :, None])
    )
    position = jnp.sum(before.astype(jnp.int32), axis=2)
    order = jnp.sum(
        jnp.where(
            position[:, None, :] == buffer_slots[None, :, None], buffer_slots[None, None, :], 0
        ),
        axis=2,
    )
    thresholds = jnp.arange(slot_count + 1, dtype=jnp.int32)
    start = jnp.sum((slot_of[:, None, :] < thresholds[None, :, None]).astype(jnp.int32), axis=2)
    slab_counts = start[:, 1:] - start[:, :-1]
    scale = 1.0 / jnp.maximum(slab_counts, 1).astype(F32)
    average = place_pieces(arrived, order, start, scale)
    average = average.reshape(chips, slab_depth, plane_rows, plane_columns)

    kernel = psf_taps / jnp.sum(psf_taps, axis=2, keepdims=True)
    own_kernel = of_own_views(kernel)
    own_shift = of_own_views(psf_shift)
    own_offset = of_own_views(background)
    wide_depth = slab_depth + 2 * EDGE

    def bands(one_kernel, one_shift):
        return (
            band_matrix(one_kernel[0], one_shift[0], slab_depth, wide_depth, EDGE).astype(BF16),
            band_matrix(one_kernel[1], one_shift[1], plane_rows, plane_rows, 0).astype(BF16),
            band_matrix(one_kernel[2], one_shift[2], plane_columns, plane_columns, 0).astype(BF16),
        )

    depth_bands, row_bands, column_bands = jax.vmap(bands)(own_kernel, own_shift)
    depth_bands = depth_bands.reshape(chips * slab_depth, wide_depth)
    banded = {
        "offset": own_offset,
        "depth": depth_bands,
        "depth_back": depth_bands.T,
        "rows": row_bands,
        "rows_back": jnp.swapaxes(row_bands, 1, 2),
        "columns": jnp.swapaxes(column_bands, 1, 2),
        "columns_back": column_bands,
    }

    global_slot = targets * slot_count + slots
    slot_total = block_count * slot_count
    counts_all = jnp.sum(
        (
            global_slot.reshape(view_count, slot_total)[:, :, None]
            == jnp.arange(slot_total, dtype=jnp.int32)[None, None, :]
        ).astype(jnp.int32),
        axis=1,
    )
    plane_mask = jnp.repeat((counts_all > 0).astype(F32), piece_depth, axis=1)
    padded_mask = jnp.pad(plane_mask, ((0, 0), (HALO, HALO)))
    window = lax.dynamic_slice_in_dim(padded_mask, my_block * slab_depth, slab_depth + 2 * HALO, 1)

    def depth_adjoint(one_kernel, one_shift):
        return band_matrix(one_kernel, one_shift, slab_depth + 2 * HALO, slab_depth, -HALO).T

    adjoint_all = jax.vmap(depth_adjoint)(kernel[:, 0], psf_shift[:, 0])
    weight_depth = jnp.einsum("vze,ve->vz", adjoint_all, window, precision=HIGHEST)
    weight_rows = column_sums(kernel[:, 1], psf_shift[:, 1], plane_rows)
    weight_columns = column_sums(kernel[:, 2], psf_shift[:, 2], plane_columns)
    weight_columns = lax.dynamic_slice_in_dim(weight_columns, my_core * LANES, LANES, 1)
    weight = 0.0
    for view in range(view_count):
        weight = weight + (
            weight_depth[view][:, None, None]
            * (weight_rows[view][:, None] * weight_columns[view][None, :])[None]
        )
    floor_weight = jnp.maximum(weight, 1.0)

    up = [(i, i + 1) for i in range(block_count - 1)]
    down = [(i + 1, i) for i in range(block_count - 1)]
    swap = [(v, v + 1 - 2 * (v % CORES)) for v in range(view_count)]

    def widen(cells):
        low = lax.ppermute(cells[slab_depth - HALO :], "block", up)
        high = lax.ppermute(cells[:HALO], "block", down)
        blank = jnp.zeros((EDGE - HALO,) + cells.shape[1:], cells.dtype)
        return jnp.concatenate([blank, low, cells, high, blank], axis=0)

    def pair(mine):
        theirs = lax.ppermute(mine, "view", swap)
        first = my_core == 0
        return jnp.where(first, mine, theirs), jnp.where(first, theirs, mine)

    def half(cells, core):
        return lax.dynamic_index_in_dim(cells, core, 0, keepdims=False)

    share = lax.dynamic_slice_in_dim(estimate0, my_core * LANES, LANES, 2)
    for iteration in range(ITERS):
        if iteration == 0:
            middle = first_half(split_columns(widen(estimate0.astype(BF16))), banded)
            spread = second_half(middle, average, banded)
        else:
            wide = jnp.stack(pair(widen(share.astype(BF16))))
            spread = whole_step(wide, average, banded)
        total = half(spread, my_core) + lax.ppermute(half(spread, 1 - my_core), "view", swap)
        from_low = lax.ppermute(
            total[slab_depth + EDGE : slab_depth + EDGE + HALO].astype(BF16), "block", up
        ).astype(F32)
        from_high = lax.ppermute(
            total[EDGE - HALO : EDGE].astype(BF16), "block", down
        ).astype(F32)
        summed = total[EDGE : EDGE + slab_depth]
        summed = summed + jnp.concatenate(
            [
                from_low,
                jnp.zeros((slab_depth - 2 * HALO,) + from_low.shape[1:], F32),
                from_high,
            ],
            axis=0,
        )
        share = share * summed / floor_weight
    return jnp.concatenate(pair(share), axis=2)


def solution(mesh):
    return jax.shard_map(
        shards,
        mesh=mesh,
        in_specs=(
            P("block", None, None),
            P("view", "block", None, None, None),
            P(),
            P(),
            P(),
            P(),
            P(),
        ),
        out_specs=P("block", None, None),
        check_vma=False,
    )
```

```python
import jax
import jax.numpy as jnp
from jax import lax
from jax.experimental import pallas as pl
from jax.experimental.pallas import tpu as pltpu
from jax.sharding import PartitionSpec as P

CAP = 2
ITERS = 2
HALO = 13
EDGE = 16
CORES = 2
LANES = 128

HIGHEST = lax.Precision.HIGHEST
BF16 = jnp.bfloat16
F32 = jnp.float32


def band_matrix(kernel, shift, row_count, column_count, lead_offset):
    tap_count = kernel.shape[0]
    radius = (tap_count - 1) // 2
    difference = (
        lax.broadcasted_iota(jnp.int32, (row_count, column_count), 1)
        - lax.broadcasted_iota(jnp.int32, (row_count, column_count), 0)
        - lead_offset
        - shift
        + radius
    )
    band = jnp.zeros((row_count, column_count), F32)
    for tap in range(tap_count):
        band = jnp.where(difference == tap, kernel[tap], band)
    return band


def column_sums(kernel, shift, length):
    tap_count = kernel.shape[-1]
    radius = (tap_count - 1) // 2
    source = (
        jnp.arange(length, dtype=jnp.int32)[None, :, None]
        - shift[:, None, None]
        - jnp.arange(tap_count, dtype=jnp.int32)[None, None, :]
        + radius
    )
    inside = (source >= 0) & (source < length)
    return jnp.sum(jnp.where(inside, kernel[:, None, :], 0.0), axis=2)


def pick_body(index_ref, piece_ref, *out_refs):
    for part, out_ref in enumerate(out_refs):
        for i in range(out_ref.shape[0]):
            out_ref[i] = piece_ref[index_ref[i * CAP + part]]


def pick_pieces(pieces, index):
    shape = (index.shape[0] // CAP,) + pieces.shape[1:]
    return pl.pallas_call(
        pick_body,
        in_specs=[pl.BlockSpec(memory_space=pltpu.SMEM), pl.BlockSpec(memory_space=pltpu.VMEM)],
        out_specs=[pl.BlockSpec(memory_space=pltpu.VMEM)] * CAP,
        out_shape=[jax.ShapeDtypeStruct(shape, pieces.dtype)] * CAP,
        compiler_params=pltpu.CompilerParams(vmem_limit_bytes=48 * 2**20),
        name="pick_pieces",
    )(index, pieces)


def place_body(order_ref, start_ref, scale_ref, incoming_ref, out_ref):
    view, step = pl.program_id(0), pl.program_id(1)
    group = out_ref.shape[1]
    for i in range(group):
        slot = step * group + i
        out_ref[0, i] = jnp.zeros(out_ref.shape[2:], F32)

        def add(k, carry):
            out_ref[0, i] += incoming_ref[0, order_ref[view, k]].astype(F32)
            return carry

        lax.fori_loop(start_ref[view, slot], start_ref[view, slot + 1], add, 0)
        out_ref[0, i] = out_ref[0, i] * scale_ref[view, slot]


def place_pieces(incoming, order, start, scale):
    views, slots = scale.shape
    tail = incoming.shape[2:]
    group = 4 if slots % 4 == 0 else 1
    return pl.pallas_call(
        place_body,
        grid=(views, slots // group),
        in_specs=[
            pl.BlockSpec(memory_space=pltpu.SMEM),
            pl.BlockSpec(memory_space=pltpu.SMEM),
            pl.BlockSpec(memory_space=pltpu.SMEM),
            pl.BlockSpec((1,) + incoming.shape[1:], lambda v, t: (v, 0, 0, 0)),
        ],
        out_specs=pl.BlockSpec((1, group) + tail, lambda v, t: (v, t, 0, 0)),
        out_shape=jax.ShapeDtypeStruct((views, slots) + tail, F32),
        compiler_params=pltpu.CompilerParams(vmem_limit_bytes=48 * 2**20),
        name="place_pieces",
    )(order, start, scale, incoming)


def split_columns(volume):
    return jnp.stack(jnp.split(volume, volume.shape[-1] // LANES, axis=-1))


def take_rows(ref, y, rows):
    halves, total = ref.shape[:2]
    return jnp.concatenate(
        [ref[h, pl.ds(y, total // rows, stride=rows), :].astype(BF16) for h in range(halves)],
        axis=1,
    )


def blur_depth_columns(depth_ref, columns_ref, volume_ref, source, middle):
    halves, depth_in, rows, _ = volume_ref.shape
    views = columns_ref.shape[0]
    depth = depth_ref.shape[0] // views
    for h in range(halves):

        def widen(z, carry):
            span = pl.ds(pl.multiple_of(z * rows, rows), rows)
            source[h, span, :] = volume_ref[h, z].astype(F32)
            return carry

        lax.fori_loop(0, depth_in, widen, 0, unroll=8)

    def row(y, carry):
        column = take_rows(source, y, rows)
        deep = jnp.dot(depth_ref[...], column, preferred_element_type=F32).astype(BF16)
        for v in range(views):
            cells = jnp.dot(
                deep[v * depth : (v + 1) * depth], columns_ref[v], preferred_element_type=F32
            )
            for h in range(halves):
                middle[v, h, pl.ds(y, depth, stride=rows), :] = cells[:, h * LANES : (h + 1) * LANES]
        return carry

    lax.fori_loop(0, rows, row, 0, unroll=4)


def spread_quotients(
    offset_ref, depth_ref, rows_ref, rows_back_ref, columns_ref, average_ref, middle, turned, out_ref
):
    views, depth, rows, _ = average_ref.shape
    halves = out_ref.shape[0]
    depth_out = out_ref.shape[1] // rows

    def plane(z, carry):
        span = pl.ds(pl.multiple_of(z * rows, rows), rows)
        for v in range(views):
            cells = jnp.concatenate(
                [middle[v, h, span, :].astype(BF16) for h in range(halves)], axis=1
            )
            blurred = jnp.dot(rows_ref[v], cells, preferred_element_type=F32) + offset_ref[v]
            quotient = (average_ref[v, z] / blurred).astype(BF16)
            cells = jnp.dot(rows_back_ref[v], quotient, preferred_element_type=F32)
            for h in range(halves):
                turned[v, h, span, :] = cells[:, h * LANES : (h + 1) * LANES]
        return carry

    lax.fori_loop(0, depth, plane, 0, unroll=4)

    def row(y, carry):
        columns = [
            jnp.dot(
                take_rows(turned.at[v], y, rows), columns_ref[v], preferred_element_type=F32
            ).astype(BF16)
            for v in range(views)
        ]
        cells = jnp.dot(
            depth_ref[...], jnp.concatenate(columns, axis=0), preferred_element_type=F32
        )
        for h in range(halves):
            out_ref[h, pl.ds(y, depth_out, stride=rows), :] = cells[:, h * LANES : (h + 1) * LANES]
        return carry

    lax.fori_loop(0, rows, row, 0, unroll=4)


def whole_step_body(
    offset_ref, depth_ref, depth_back_ref, rows_ref, rows_back_ref, columns_ref, columns_back_ref,
    average_ref, volume_ref, out_ref, source, middle,
):
    blur_depth_columns(depth_ref, columns_ref, volume_ref, source, middle)
    spread_quotients(
        offset_ref, depth_back_ref, rows_ref, rows_back_ref, columns_back_ref, average_ref,
        middle, middle, out_ref,
    )


IN_SMEM = pl.BlockSpec(memory_space=pltpu.SMEM)
IN_VMEM = pl.BlockSpec(memory_space=pltpu.VMEM)
ROOM = pltpu.CompilerParams(vmem_limit_bytes=60 * 2**20)


def first_half(volume, bands):
    halves, depth_in, rows, _ = volume.shape
    views = bands["columns"].shape[0]
    depth = bands["depth"].shape[0] // views
    shape = (views, halves, depth * rows, LANES)
    width = halves * LANES
    return pl.pallas_call(
        blur_depth_columns,
        in_specs=[IN_VMEM] * 3,
        out_specs=[IN_VMEM] * 2,
        out_shape=[
            jax.ShapeDtypeStruct((halves, depth_in * rows, LANES), F32),
            jax.ShapeDtypeStruct(shape, F32),
        ],
        compiler_params=ROOM,
        cost_estimate=pl.CostEstimate(
            flops=8 * views * depth * rows * width * (depth_in + width),
            bytes_accessed=4 * (views * depth + depth_in) * rows * width,
            transcendentals=0,
        ),
        name="blur_depth_columns",
    )(bands["depth"], bands["columns"], volume)[1]


def second_half(middle, average, bands):
    views, halves, _, _ = middle.shape
    rows = average.shape[2]
    depth_out = bands["depth_back"].shape[0]
    return pl.pallas_call(
        spread_quotients_apart,
        in_specs=[IN_SMEM] + [IN_VMEM] * 6,
        out_specs=IN_VMEM,
        out_shape=jax.ShapeDtypeStruct((halves, depth_out * rows, LANES), F32),
        scratch_shapes=[pltpu.VMEM(middle.shape, F32)],
        compiler_params=ROOM,
        name="spread_quotients",
    )(
        bands["offset"], bands["depth_back"], bands["rows"], bands["rows_back"],
        bands["columns_back"], average, middle,
    ).reshape(halves, depth_out, rows, LANES)


def spread_quotients_apart(
    offset_ref, depth_ref, rows_ref, rows_back_ref, columns_ref, average_ref, middle, out_ref, turned
):
    spread_quotients(
        offset_ref, depth_ref, rows_ref, rows_back_ref, columns_ref, average_ref, middle, turned,
        out_ref,
    )


def whole_step(volume, average, bands):
    halves, depth_in, rows, _ = volume.shape
    views, depth = average.shape[:2]
    depth_out = bands["depth_back"].shape[0]
    return pl.pallas_call(
        whole_step_body,
        in_specs=[IN_SMEM] + [IN_VMEM] * 8,
        out_specs=IN_VMEM,
        out_shape=jax.ShapeDtypeStruct((halves, depth_out * rows, LANES), F32),
        scratch_shapes=[
            pltpu.VMEM((halves, depth_in * rows, LANES), F32),
            pltpu.VMEM((views, halves, depth * rows, LANES), F32),
        ],
        compiler_params=ROOM,
        name="whole_step",
    )(
        bands["offset"], bands["depth"], bands["depth_back"], bands["rows"], bands["rows_back"],
        bands["columns"], bands["columns_back"], average, volume,
    ).reshape(halves, depth_out, rows, LANES)


def shards(estimate0, pieces, dest_block, slot_index, psf_shift, psf_taps, background):
    block_count = lax.axis_size("block")
    view_count = lax.axis_size("view")
    my_view = lax.axis_index("view")
    my_block = lax.axis_index("block")
    slab_depth, plane_rows, plane_columns = estimate0.shape
    slot_count = pieces.shape[1]
    piece_depth = pieces.shape[2]
    chips = view_count // CORES
    my_core = lax.rem(my_view, CORES)

    def of_own_views(cells):
        return jnp.concatenate(
            [
                lax.dynamic_slice_in_dim(cells, lax.rem(my_view + CORES * hop, view_count), 1, 0)
                for hop in range(chips)
            ]
        )

    targets = dest_block[:, :, 0].reshape(view_count, block_count, slot_count)
    slots = slot_index.reshape(view_count, block_count, slot_count)
    earlier = lax.broadcasted_iota(jnp.int32, (slot_count, slot_count), 1) < lax.broadcasted_iota(
        jnp.int32, (slot_count, slot_count), 0
    )
    here = lax.dynamic_slice(targets, (my_view, my_block, 0), (1, 1, slot_count))[0, 0]
    here_rank = jnp.sum(((here[:, None] == here[None, :]) & earlier).astype(jnp.int32), axis=1)
    buffer_slots = jnp.arange(block_count * CAP, dtype=jnp.int32)
    hit = buffer_slots[:, None] == (here * CAP + here_rank)[None, :]
    pick = jnp.sum(
        jnp.where(hit, lax.broadcasted_iota(jnp.int32, hit.shape, 1), 0), axis=1
    )
    outgoing = pick_pieces(
        pieces.reshape(slot_count, piece_depth * plane_rows, plane_columns), pick
    )
    parts = [[] for _ in range(chips)]
    for part in range(CAP):
        incoming = lax.all_to_all(outgoing[part], "block", split_axis=0, concat_axis=0, tiled=True)
        parts[0].append(incoming)
        for hop in range(1, chips):
            parts[hop].append(
                lax.ppermute(
                    incoming,
                    "view",
                    [((v + CORES * hop) % view_count, v) for v in range(view_count)],
                )
            )
    arrived = jnp.stack([jnp.concatenate(group, axis=0) for group in parts])

    view_targets = of_own_views(targets)
    view_slots = of_own_views(slots)
    ranks = jnp.sum(
        ((view_targets[..., :, None] == view_targets[..., None, :]) & earlier).astype(jnp.int32),
        axis=-1,
    )
    column = jnp.where(
        view_targets == my_block,
        ranks * block_count + lax.broadcasted_iota(jnp.int32, view_targets.shape, 1),
        -1,
    )
    matches = column[..., None] == buffer_slots
    slot_of = jnp.sum(jnp.where(matches, view_slots[..., None] + 1, 0), axis=(1, 2)) - 1
    slot_of = jnp.where(slot_of < 0, slot_count, slot_of)
    before = (slot_of[:, None, :] < slot_of[:, :, None]) | (
        (slot_of[:, None, :] == slot_of[:, :, None])
        & (buffer_slots[None, None, :] < buffer_slots[None, :, None])
    )
    position = jnp.sum(before.astype(jnp.int32), axis=2)
    order = jnp.sum(
        jnp.where(
            position[:, None, :] == buffer_slots[None, :, None], buffer_slots[None, None, :], 0
        ),
        axis=2,
    )
    thresholds = jnp.arange(slot_count + 1, dtype=jnp.int32)
    start = jnp.sum((slot_of[:, None, :] < thresholds[None, :, None]).astype(jnp.int32), axis=2)
    slab_counts = start[:, 1:] - start[:, :-1]
    scale = 1.0 / jnp.maximum(slab_counts, 1).astype(F32)
    average = place_pieces(arrived, order, start, scale)
    average = average.reshape(chips, slab_depth, plane_rows, plane_columns)

    kernel = psf_taps / jnp.sum(psf_taps, axis=2, keepdims=True)
    own_kernel = of_own_views(kernel)
    own_shift = of_own_views(psf_shift)
    own_offset = of_own_views(background)
    wide_depth = slab_depth + 2 * EDGE

    def bands(one_kernel, one_shift):
        return (
            band_matrix(one_kernel[0], one_shift[0], slab_depth, wide_depth, EDGE).astype(BF16),
            band_matrix(one_kernel[1], one_shift[1], plane_rows, plane_rows, 0).astype(BF16),
            band_matrix(one_kernel[2], one_shift[2], plane_columns, plane_columns, 0).astype(BF16),
        )

    depth_bands, row_bands, column_bands = jax.vmap(bands)(own_kernel, own_shift)
    depth_bands = depth_bands.reshape(chips * slab_depth, wide_depth)
    banded = {
        "offset": own_offset,
        "depth": depth_bands,
        "depth_back": depth_bands.T,
        "rows": row_bands,
        "rows_back": jnp.swapaxes(row_bands, 1, 2),
        "columns": jnp.swapaxes(column_bands, 1, 2),
        "columns_back": column_bands,
    }

    global_slot = targets * slot_count + slots
    slot_total = block_count * slot_count
    counts_all = jnp.sum(
        (
            global_slot.reshape(view_count, slot_total)[:, :, None]
            == jnp.arange(slot_total, dtype=jnp.int32)[None, None, :]
        ).astype(jnp.int32),
        axis=1,
    )
    plane_mask = jnp.repeat((counts_all > 0).astype(F32), piece_depth, axis=1)
    padded_mask = jnp.pad(plane_mask, ((0, 0), (HALO, HALO)))
    window = lax.dynamic_slice_in_dim(padded_mask, my_block * slab_depth, slab_depth + 2 * HALO, 1)

    def depth_adjoint(one_kernel, one_shift):
        return band_matrix(one_kernel, one_shift, slab_depth + 2 * HALO, slab_depth, -HALO).T

    adjoint_all = jax.vmap(depth_adjoint)(kernel[:, 0], psf_shift[:, 0])
    weight_depth = jnp.einsum("vze,ve->vz", adjoint_all, window, precision=HIGHEST)
    weight_rows = column_sums(kernel[:, 1], psf_shift[:, 1], plane_rows)
    weight_columns = column_sums(kernel[:, 2], psf_shift[:, 2], plane_columns)
    weight_columns = lax.dynamic_slice_in_dim(weight_columns, my_core * LANES, LANES, 1)
    weight = 0.0
    for view in range(view_count):
        weight = weight + (
            weight_depth[view][:, None, None]
            * (weight_rows[view][:, None] * weight_columns[view][None, :])[None]
        )
    floor_weight = jnp.maximum(weight, 1.0)

    up = [(i, i + 1) for i in range(block_count - 1)]
    down = [(i + 1, i) for i in range(block_count - 1)]
    swap = [(v, v + 1 - 2 * (v % CORES)) for v in range(view_count)]

    def widen(cells):
        low = lax.ppermute(cells[slab_depth - HALO :], "block", up)
        high = lax.ppermute(cells[:HALO], "block", down)
        blank = jnp.zeros((EDGE - HALO,) + cells.shape[1:], cells.dtype)
        return jnp.concatenate([blank, low, cells, high, blank], axis=0)

    def pair(mine):
        theirs = lax.ppermute(mine, "view", swap)
        first = my_core == 0
        return jnp.where(first, mine, theirs), jnp.where(first, theirs, mine)

    def half(cells, core):
        return lax.dynamic_index_in_dim(cells, core, 0, keepdims=False)

    share = lax.dynamic_slice_in_dim(estimate0, my_core * LANES, LANES, 2)
    for iteration in range(ITERS):
        if iteration == 0:
            middle = first_half(split_columns(widen(estimate0.astype(BF16))), banded)
            spread = second_half(middle, average, banded)
        else:
            wide = jnp.stack(pair(widen(share.astype(BF16))))
            spread = whole_step(wide, average, banded)
        total = half(spread, my_core) + lax.ppermute(half(spread, 1 - my_core), "view", swap)
        from_low = lax.ppermute(
            total[slab_depth + EDGE : slab_depth + EDGE + HALO].astype(BF16), "block", up
        ).astype(F32)
        from_high = lax.ppermute(
            total[EDGE - HALO : EDGE].astype(BF16), "block", down
        ).astype(F32)
        summed = total[EDGE : EDGE + slab_depth]
        summed = summed + jnp.concatenate(
            [
                from_low,
                jnp.zeros((slab_depth - 2 * HALO,) + from_low.shape[1:], F32),
                from_high,
            ],
            axis=0,
        )
        share = share * summed / floor_weight
    return jnp.concatenate(pair(share), axis=2)


def solution(mesh):
    return jax.shard_map(
        shards,
        mesh=mesh,
        in_specs=(
            P("block", None, None),
            P("view", "block", None, None, None),
            P(),
            P(),
            P(),
            P(),
            P(),
        ),
        out_specs=P("block", None, None),
        check_vma=False,
    )
```

```python
import jax
import jax.numpy as jnp
from jax import lax
from jax.experimental import pallas as pl
from jax.experimental.pallas import tpu as pltpu
from jax.sharding import PartitionSpec as P

CAP = 2
ITERS = 2
HALO = 13
EDGE = 16
CORES = 2
LANES = 128

HIGHEST = lax.Precision.HIGHEST
BF16 = jnp.bfloat16
F32 = jnp.float32


def band_matrix(kernel, shift, row_count, column_count, lead_offset):
    tap_count = kernel.shape[0]
    radius = (tap_count - 1) // 2
    difference = (
        lax.broadcasted_iota(jnp.int32, (row_count, column_count), 1)
        - lax.broadcasted_iota(jnp.int32, (row_count, column_count), 0)
        - lead_offset
        - shift
        + radius
    )
    band = jnp.zeros((row_count, column_count), F32)
    for tap in range(tap_count):
        band = jnp.where(difference == tap, kernel[tap], band)
    return band


def column_sums(kernel, shift, length):
    tap_count = kernel.shape[-1]
    radius = (tap_count - 1) // 2
    source = (
        jnp.arange(length, dtype=jnp.int32)[None, :, None]
        - shift[:, None, None]
        - jnp.arange(tap_count, dtype=jnp.int32)[None, None, :]
        + radius
    )
    inside = (source >= 0) & (source < length)
    return jnp.sum(jnp.where(inside, kernel[:, None, :], 0.0), axis=2)


def pick_body(index_ref, piece_ref, *out_refs):
    for part, out_ref in enumerate(out_refs):
        for i in range(out_ref.shape[0]):
            out_ref[i] = piece_ref[index_ref[i * CAP + part]]


def pick_pieces(pieces, index):
    shape = (index.shape[0] // CAP,) + pieces.shape[1:]
    return pl.pallas_call(
        pick_body,
        in_specs=[pl.BlockSpec(memory_space=pltpu.SMEM), pl.BlockSpec(memory_space=pltpu.VMEM)],
        out_specs=[pl.BlockSpec(memory_space=pltpu.VMEM)] * CAP,
        out_shape=[jax.ShapeDtypeStruct(shape, pieces.dtype)] * CAP,
        compiler_params=pltpu.CompilerParams(vmem_limit_bytes=48 * 2**20),
        name="pick_pieces",
    )(index, pieces)


def place_body(order_ref, start_ref, scale_ref, incoming_ref, out_ref):
    view, step = pl.program_id(0), pl.program_id(1)
    group = out_ref.shape[1]
    for i in range(group):
        slot = step * group + i
        out_ref[0, i] = jnp.zeros(out_ref.shape[2:], F32)

        def add(k, carry):
            out_ref[0, i] += incoming_ref[0, order_ref[view, k]].astype(F32)
            return carry

        lax.fori_loop(start_ref[view, slot], start_ref[view, slot + 1], add, 0)
        out_ref[0, i] = out_ref[0, i] * scale_ref[view, slot]


def place_pieces(incoming, order, start, scale):
    views, slots = scale.shape
    tail = incoming.shape[2:]
    group = 4 if slots % 4 == 0 else 1
    return pl.pallas_call(
        place_body,
        grid=(views, slots // group),
        in_specs=[
            pl.BlockSpec(memory_space=pltpu.SMEM),
            pl.BlockSpec(memory_space=pltpu.SMEM),
            pl.BlockSpec(memory_space=pltpu.SMEM),
            pl.BlockSpec((1,) + incoming.shape[1:], lambda v, t: (v, 0, 0, 0)),
        ],
        out_specs=pl.BlockSpec((1, group) + tail, lambda v, t: (v, t, 0, 0)),
        out_shape=jax.ShapeDtypeStruct((views, slots) + tail, F32),
        compiler_params=pltpu.CompilerParams(vmem_limit_bytes=48 * 2**20),
        name="place_pieces",
    )(order, start, scale, incoming)


def split_columns(volume):
    return jnp.stack(jnp.split(volume, volume.shape[-1] // LANES, axis=-1))


def take_rows(ref, y, rows):
    halves, total = ref.shape[:2]
    return jnp.concatenate(
        [ref[h, pl.ds(y, total // rows, stride=rows), :].astype(BF16) for h in range(halves)],
        axis=1,
    )


def blur_depth_columns(depth_ref, columns_ref, volume_ref, source, middle):
    halves, depth_in, rows, _ = volume_ref.shape
    views = columns_ref.shape[0]
    depth = depth_ref.shape[0] // views
    for h in range(halves):

        def widen(z, carry):
            span = pl.ds(pl.multiple_of(z * rows, rows), rows)
            source[h, span, :] = volume_ref[h, z].astype(F32)
            return carry

        lax.fori_loop(0, depth_in, widen, 0, unroll=8)

    def row(y, carry):
        column = take_rows(source, y, rows)
        deep = jnp.dot(depth_ref[...], column, preferred_element_type=F32).astype(BF16)
        for v in range(views):
            cells = jnp.dot(
                deep[v * depth : (v + 1) * depth], columns_ref[v], preferred_element_type=F32
            )
            for h in range(halves):
                middle[v, h, pl.ds(y, depth, stride=rows), :] = cells[:, h * LANES : (h + 1) * LANES]
        return carry

    lax.fori_loop(0, rows, row, 0, unroll=16)


def spread_quotients(
    offset_ref, depth_ref, rows_ref, rows_back_ref, columns_ref, average_ref, middle, turned, out_ref
):
    views, depth, rows, _ = average_ref.shape
    halves = out_ref.shape[0]
    depth_out = out_ref.shape[1] // rows

    def plane(z, carry):
        span = pl.ds(pl.multiple_of(z * rows, rows), rows)
        for v in range(views):
            cells = jnp.concatenate(
                [middle[v, h, span, :].astype(BF16) for h in range(halves)], axis=1
            )
            blurred = jnp.dot(rows_ref[v], cells, preferred_element_type=F32) + offset_ref[v]
            quotient = (average_ref[v, z] / blurred).astype(BF16)
            cells = jnp.dot(rows_back_ref[v], quotient, preferred_element_type=F32)
            for h in range(halves):
                turned[v, h, span, :] = cells[:, h * LANES : (h + 1) * LANES]
        return carry

    lax.fori_loop(0, depth, plane, 0, unroll=16)

    def row(y, carry):
        columns = [
            jnp.dot(
                take_rows(turned.at[v], y, rows), columns_ref[v], preferred_element_type=F32
            ).astype(BF16)
            for v in range(views)
        ]
        cells = jnp.dot(
            depth_ref[...], jnp.concatenate(columns, axis=0), preferred_element_type=F32
        )
        for h in range(halves):
            out_ref[h, pl.ds(y, depth_out, stride=rows), :] = cells[:, h * LANES : (h + 1) * LANES]
        return carry

    lax.fori_loop(0, rows, row, 0, unroll=16)


def whole_step_body(
    offset_ref, depth_ref, depth_back_ref, rows_ref, rows_back_ref, columns_ref, columns_back_ref,
    average_ref, volume_ref, out_ref, source, middle,
):
    blur_depth_columns(depth_ref, columns_ref, volume_ref, source, middle)
    spread_quotients(
        offset_ref, depth_back_ref, rows_ref, rows_back_ref, columns_back_ref, average_ref,
        middle, middle, out_ref,
    )


IN_SMEM = pl.BlockSpec(memory_space=pltpu.SMEM)
IN_VMEM = pl.BlockSpec(memory_space=pltpu.VMEM)
ROOM = pltpu.CompilerParams(vmem_limit_bytes=60 * 2**20)


def first_half(volume, bands):
    halves, depth_in, rows, _ = volume.shape
    views = bands["columns"].shape[0]
    depth = bands["depth"].shape[0] // views
    shape = (views, halves, depth * rows, LANES)
    width = halves * LANES
    return pl.pallas_call(
        blur_depth_columns,
        in_specs=[IN_VMEM] * 3,
        out_specs=[IN_VMEM] * 2,
        out_shape=[
            jax.ShapeDtypeStruct((halves, depth_in * rows, LANES), F32),
            jax.ShapeDtypeStruct(shape, F32),
        ],
        compiler_params=ROOM,
        cost_estimate=pl.CostEstimate(
            flops=8 * views * depth * rows * width * (depth_in + width),
            bytes_accessed=4 * (views * depth + depth_in) * rows * width,
            transcendentals=0,
        ),
        name="blur_depth_columns",
    )(bands["depth"], bands["columns"], volume)[1]


def second_half(middle, average, bands):
    views, halves, _, _ = middle.shape
    rows = average.shape[2]
    depth_out = bands["depth_back"].shape[0]
    return pl.pallas_call(
        spread_quotients_apart,
        in_specs=[IN_SMEM] + [IN_VMEM] * 6,
        out_specs=IN_VMEM,
        out_shape=jax.ShapeDtypeStruct((halves, depth_out * rows, LANES), F32),
        scratch_shapes=[pltpu.VMEM(middle.shape, F32)],
        compiler_params=ROOM,
        name="spread_quotients",
    )(
        bands["offset"], bands["depth_back"], bands["rows"], bands["rows_back"],
        bands["columns_back"], average, middle,
    ).reshape(halves, depth_out, rows, LANES)


def spread_quotients_apart(
    offset_ref, depth_ref, rows_ref, rows_back_ref, columns_ref, average_ref, middle, out_ref, turned
):
    spread_quotients(
        offset_ref, depth_ref, rows_ref, rows_back_ref, columns_ref, average_ref, middle, turned,
        out_ref,
    )


def whole_step(volume, average, bands):
    halves, depth_in, rows, _ = volume.shape
    views, depth = average.shape[:2]
    depth_out = bands["depth_back"].shape[0]
    return pl.pallas_call(
        whole_step_body,
        in_specs=[IN_SMEM] + [IN_VMEM] * 8,
        out_specs=IN_VMEM,
        out_shape=jax.ShapeDtypeStruct((halves, depth_out * rows, LANES), F32),
        scratch_shapes=[
            pltpu.VMEM((halves, depth_in * rows, LANES), F32),
            pltpu.VMEM((views, halves, depth * rows, LANES), F32),
        ],
        compiler_params=ROOM,
        name="whole_step",
    )(
        bands["offset"], bands["depth"], bands["depth_back"], bands["rows"], bands["rows_back"],
        bands["columns"], bands["columns_back"], average, volume,
    ).reshape(halves, depth_out, rows, LANES)


def shards(estimate0, pieces, dest_block, slot_index, psf_shift, psf_taps, background):
    block_count = lax.axis_size("block")
    view_count = lax.axis_size("view")
    my_view = lax.axis_index("view")
    my_block = lax.axis_index("block")
    slab_depth, plane_rows, plane_columns = estimate0.shape
    slot_count = pieces.shape[1]
    piece_depth = pieces.shape[2]
    chips = view_count // CORES
    my_core = lax.rem(my_view, CORES)

    def of_own_views(cells):
        return jnp.concatenate(
            [
                lax.dynamic_slice_in_dim(cells, lax.rem(my_view + CORES * hop, view_count), 1, 0)
                for hop in range(chips)
            ]
        )

    targets = dest_block[:, :, 0].reshape(view_count, block_count, slot_count)
    slots = slot_index.reshape(view_count, block_count, slot_count)
    earlier = lax.broadcasted_iota(jnp.int32, (slot_count, slot_count), 1) < lax.broadcasted_iota(
        jnp.int32, (slot_count, slot_count), 0
    )
    here = lax.dynamic_slice(targets, (my_view, my_block, 0), (1, 1, slot_count))[0, 0]
    here_rank = jnp.sum(((here[:, None] == here[None, :]) & earlier).astype(jnp.int32), axis=1)
    buffer_slots = jnp.arange(block_count * CAP, dtype=jnp.int32)
    hit = buffer_slots[:, None] == (here * CAP + here_rank)[None, :]
    pick = jnp.sum(
        jnp.where(hit, lax.broadcasted_iota(jnp.int32, hit.shape, 1), 0), axis=1
    )
    outgoing = pick_pieces(
        pieces.reshape(slot_count, piece_depth * plane_rows, plane_columns), pick
    )
    parts = [[] for _ in range(chips)]
    for part in range(CAP):
        incoming = lax.all_to_all(outgoing[part], "block", split_axis=0, concat_axis=0, tiled=True)
        parts[0].append(incoming)
        for hop in range(1, chips):
            parts[hop].append(
                lax.ppermute(
                    incoming,
                    "view",
                    [((v + CORES * hop) % view_count, v) for v in range(view_count)],
                )
            )
    arrived = jnp.stack([jnp.concatenate(group, axis=0) for group in parts])

    view_targets = of_own_views(targets)
    view_slots = of_own_views(slots)
    ranks = jnp.sum(
        ((view_targets[..., :, None] == view_targets[..., None, :]) & earlier).astype(jnp.int32),
        axis=-1,
    )
    column = jnp.where(
        view_targets == my_block,
        ranks * block_count + lax.broadcasted_iota(jnp.int32, view_targets.shape, 1),
        -1,
    )
    matches = column[..., None] == buffer_slots
    slot_of = jnp.sum(jnp.where(matches, view_slots[..., None] + 1, 0), axis=(1, 2)) - 1
    slot_of = jnp.where(slot_of < 0, slot_count, slot_of)
    before = (slot_of[:, None, :] < slot_of[:, :, None]) | (
        (slot_of[:, None, :] == slot_of[:, :, None])
        & (buffer_slots[None, None, :] < buffer_slots[None, :, None])
    )
    position = jnp.sum(before.astype(jnp.int32), axis=2)
    order = jnp.sum(
        jnp.where(
            position[:, None, :] == buffer_slots[None, :, None], buffer_slots[None, None, :], 0
        ),
        axis=2,
    )
    thresholds = jnp.arange(slot_count + 1, dtype=jnp.int32)
    start = jnp.sum((slot_of[:, None, :] < thresholds[None, :, None]).astype(jnp.int32), axis=2)
    slab_counts = start[:, 1:] - start[:, :-1]
    scale = 1.0 / jnp.maximum(slab_counts, 1).astype(F32)
    average = place_pieces(arrived, order, start, scale)
    average = average.reshape(chips, slab_depth, plane_rows, plane_columns)

    kernel = psf_taps / jnp.sum(psf_taps, axis=2, keepdims=True)
    own_kernel = of_own_views(kernel)
    own_shift = of_own_views(psf_shift)
    own_offset = of_own_views(background)
    wide_depth = slab_depth + 2 * EDGE

    def bands(one_kernel, one_shift):
        return (
            band_matrix(one_kernel[0], one_shift[0], slab_depth, wide_depth, EDGE).astype(BF16),
            band_matrix(one_kernel[1], one_shift[1], plane_rows, plane_rows, 0).astype(BF16),
            band_matrix(one_kernel[2], one_shift[2], plane_columns, plane_columns, 0).astype(BF16),
        )

    depth_bands, row_bands, column_bands = jax.vmap(bands)(own_kernel, own_shift)
    depth_bands = depth_bands.reshape(chips * slab_depth, wide_depth)
    banded = {
        "offset": own_offset,
        "depth": depth_bands,
        "depth_back": depth_bands.T,
        "rows": row_bands,
        "rows_back": jnp.swapaxes(row_bands, 1, 2),
        "columns": jnp.swapaxes(column_bands, 1, 2),
        "columns_back": column_bands,
    }

    global_slot = targets * slot_count + slots
    slot_total = block_count * slot_count
    counts_all = jnp.sum(
        (
            global_slot.reshape(view_count, slot_total)[:, :, None]
            == jnp.arange(slot_total, dtype=jnp.int32)[None, None, :]
        ).astype(jnp.int32),
        axis=1,
    )
    plane_mask = jnp.repeat((counts_all > 0).astype(F32), piece_depth, axis=1)
    padded_mask = jnp.pad(plane_mask, ((0, 0), (HALO, HALO)))
    window = lax.dynamic_slice_in_dim(padded_mask, my_block * slab_depth, slab_depth + 2 * HALO, 1)

    def depth_adjoint(one_kernel, one_shift):
        return band_matrix(one_kernel, one_shift, slab_depth + 2 * HALO, slab_depth, -HALO).T

    adjoint_all = jax.vmap(depth_adjoint)(kernel[:, 0], psf_shift[:, 0])
    weight_depth = jnp.einsum("vze,ve->vz", adjoint_all, window, precision=HIGHEST)
    weight_rows = column_sums(kernel[:, 1], psf_shift[:, 1], plane_rows)
    weight_columns = column_sums(kernel[:, 2], psf_shift[:, 2], plane_columns)
    weight_columns = lax.dynamic_slice_in_dim(weight_columns, my_core * LANES, LANES, 1)
    weight = 0.0
    for view in range(view_count):
        weight = weight + (
            weight_depth[view][:, None, None]
            * (weight_rows[view][:, None] * weight_columns[view][None, :])[None]
        )
    floor_weight = jnp.maximum(weight, 1.0)

    up = [(i, i + 1) for i in range(block_count - 1)]
    down = [(i + 1, i) for i in range(block_count - 1)]
    swap = [(v, v + 1 - 2 * (v % CORES)) for v in range(view_count)]

    def widen(cells):
        low = lax.ppermute(cells[slab_depth - HALO :], "block", up)
        high = lax.ppermute(cells[:HALO], "block", down)
        blank = jnp.zeros((EDGE - HALO,) + cells.shape[1:], cells.dtype)
        return jnp.concatenate([blank, low, cells, high, blank], axis=0)

    def pair(mine):
        theirs = lax.ppermute(mine, "view", swap)
        first = my_core == 0
        return jnp.where(first, mine, theirs), jnp.where(first, theirs, mine)

    def half(cells, core):
        return lax.dynamic_index_in_dim(cells, core, 0, keepdims=False)

    share = lax.dynamic_slice_in_dim(estimate0, my_core * LANES, LANES, 2)
    for iteration in range(ITERS):
        if iteration == 0:
            middle = first_half(split_columns(widen(estimate0.astype(BF16))), banded)
            spread = second_half(middle, average, banded)
        else:
            wide = jnp.stack(pair(widen(share.astype(BF16))))
            spread = whole_step(wide, average, banded)
        total = half(spread, my_core) + lax.ppermute(half(spread, 1 - my_core), "view", swap)
        from_low = lax.ppermute(
            total[slab_depth + EDGE : slab_depth + EDGE + HALO].astype(BF16), "block", up
        ).astype(F32)
        from_high = lax.ppermute(
            total[EDGE - HALO : EDGE].astype(BF16), "block", down
        ).astype(F32)
        summed = total[EDGE : EDGE + slab_depth]
        summed = summed + jnp.concatenate(
            [
                from_low,
                jnp.zeros((slab_depth - 2 * HALO,) + from_low.shape[1:], F32),
                from_high,
            ],
            axis=0,
        )
        share = share * summed / floor_weight
    return jnp.concatenate(pair(share), axis=2)


def solution(mesh):
    return jax.shard_map(
        shards,
        mesh=mesh,
        in_specs=(
            P("block", None, None),
            P("view", "block", None, None, None),
            P(),
            P(),
            P(),
            P(),
            P(),
        ),
        out_specs=P("block", None, None),
        check_vma=False,
    )
```
